512 devices in a mesh: dp: 16 (over z), expert: 32 (over y, x, core).
Axes of the slice: x: 4, y: 4, z: 16, core: 2. Of those that a mesh axis runs over, the one named last changes fastest.
Arguments:
- tokens: bfloat16 [4096, 4096], P('expert', 'dp'), may hold values from -6 to 6
- expert_ids: int32 [4096, 8], P('expert'), may hold values from 0 to 63, all different within a row; in each aligned block of 128 rows (0 to 127, 128 to 255, ...) at most 20 rows name the same one
- combine: float32 [4096, 8], P('expert'), may hold values from 0.05 to 0.5
- gate_weight: bfloat16 [64, 4096, 768], P('expert', 'dp'), may hold values from -0.09375 to 0.09375
- up_weight: bfloat16 [64, 4096, 768], P('expert', 'dp'), may hold values from -0.09375 to 0.09375
- down_weight: bfloat16 [64, 768, 4096], P('expert', None, 'dp'), may hold values from -0.21875 to 0.21875
Outputs:
- mixed: bfloat16 [4096, 4096], P('expert', 'dp')
The draws below stay inside these ranges and needn't reach their ends.
Inputs may be any that keep to these rules, and one draw needn't show every extreme that they name: `expert_ids`: each row names 8 different experts. In each aligned block of 128 rows (the rows of one index of expert) no expert is named by more than 20 rows, a bound that some block reaches.
All inputs are finite; a program needn't handle non-finite values.
Results may differ from the reference program's by a relative error of at most 0.0057.
Values may be sent and summed in bfloat16 or wider, within the bound.
No kernel may reach another device: no remote copies, remote signals or barrier semaphores. Data moves between devices by JAX's collectives and lax.ppermute only.
A program may use at most 64 MiB of HBM per device.

```python
import math
import jax
import jax.numpy as jnp
import numpy as np
from jax import lax

D = 4096
FF = 768
EXPERTS = 64
TOP = 8
TOK_BLK = 128
CAP = 20
TOKENS = 4096
N_EXPERT = 32


def block_levels(rng, shape, split, low, top_value):
    factor_of, own = 1.0, jax.random.fold_in(rng, 6)
    for dim, parts in split:
        steps = jnp.exp(jax.random.uniform(jax.random.fold_in(own, dim), (parts,), jnp.float32, low / len(split), top_value / len(split)))
        factor_of = factor_of * jnp.repeat(steps, shape[dim] // parts).reshape([-1 if axis == dim else 1 for axis in range(len(shape))])
    return factor_of


def assign_block(rng, own, number, rows, number_of, top, most, lean):
    order = jax.random.permutation(rng, number_of)
    packed, ordinary = load_shares(number_of, rows * top, most, lean, True), load_shares(number_of, rows * top, most, lean, False)
    places = jnp.arange(number_of)

    def named(tallies, turn):
        used = int((tallies > 0).sum())
        fixed = max(1, used // 4)
        passed = fixed + (places - fixed + turn * (used - fixed)) % max(1, number_of - fixed)
        return jnp.zeros((number_of,), jnp.int32).at[order[jnp.where(places < fixed, places, passed)]].set(jnp.asarray(tallies, jnp.int32))

    tallies = jnp.where(number % 4 == 0, named(packed, number // 4), named(ordinary, number - number // 4 - 1))
    mixed = jax.random.permutation(jax.random.fold_in(own, 3), number_of)
    donor, receiver = mixed[0:number_of // 2 * 2:2], mixed[1:number_of // 2 * 2:2]
    room = jnp.minimum(tallies[donor] - 1, most - tallies[receiver]) // 2
    room = jnp.where((donor == order[0]) | (receiver == order[0]) | (tallies[receiver] == 0), 0, jnp.maximum(room, 0))
    passed = jax.random.randint(jax.random.fold_in(own, 4), (number_of // 2,), 0, 1 << 20) % (room + 1)
    tallies = tallies.at[donor].add(-passed).at[receiver].add(passed)
    items = jnp.searchsorted(jnp.cumsum(tallies), jnp.arange(rows * top), side="right").astype(jnp.int32)
    table = items.reshape(top, rows).T
    table = table[jax.random.permutation(jax.random.fold_in(own, 1), rows)]
    turn = jax.random.randint(jax.random.fold_in(own, 2), (rows, 1), 0, top)
    return jnp.take_along_axis(table, (jnp.arange(top)[None, :] + turn) % top, axis=1)


def load_shares(amount, total, bound, skew, full):
    loads = [(1 << 20) // math.isqrt(rank ** skew) + 1 for rank in range(1, amount + 1)]
    largest = bound if full else min(bound, max(-(-total // amount), total * loads[0] // sum(loads)))
    least = 1 if total - largest >= amount - 1 else 0
    counts, spare = [largest] + [least] * (amount - 1), total - largest - least * (amount - 1)
    while spare > 0:
        candidates = [i for i in range(1, amount) if counts[i] < largest] or [i for i in range(1, amount) if counts[i] < bound]
        whole, budget = sum([loads[i] for i in candidates]), spare
        for i in candidates:
            more = min(bound - counts[i], max(1, budget * loads[i] // whole), spare)
            counts[i] = counts[i] + more
            spare = spare - more
    return np.array(counts)


def noise(stream_key, shape, spread, reach, split=(), kind=jnp.bfloat16):
    array = spread * jax.random.normal(stream_key, shape, jnp.float32)
    if split:
        array = array * block_levels(stream_key, shape, split, -0.22, 0.18)
    return jnp.clip(array, -reach, reach).astype(kind)


def setup_inputs(seed: int = 0) -> dict:
    streams_of = jax.random.split(jax.random.key(seed), 7)
    tokens = noise(streams_of[0], (TOKENS, D), 1.0, 6.0, ((0, 32), (1, 16)))
    expert_ids_keys = jax.random.split(jax.random.fold_in(streams_of[1], 1), TOKENS // TOK_BLK)
    expert_ids_turns = jax.random.permutation(jax.random.fold_in(streams_of[1], 3), TOKENS // TOK_BLK)
    expert_ids = jax.vmap(lambda own, number: assign_block(jax.random.fold_in(streams_of[1], 2), own, number, TOK_BLK, EXPERTS, TOP, CAP, 2))(expert_ids_keys, expert_ids_turns).reshape((TOKENS, TOP))
    combine = jnp.clip(jnp.exp(math.log(0.5) - 2.3025851 * jax.random.uniform(streams_of[2], (TOKENS, TOP), jnp.float32) ** block_levels(streams_of[2], (TOKENS, TOP), ((0, 32),), -0.2, 0.2)), 0.05, 0.5)
    gate_weight = noise(streams_of[3], (EXPERTS, D, FF), D ** -0.5, 0.09375, ((0, 32), (1, 16)))
    up_weight = noise(streams_of[4], (EXPERTS, D, FF), D ** -0.5, 0.09375, ((0, 32), (1, 16)))
    down_weight = noise(streams_of[5], (EXPERTS, FF, D), FF ** -0.5, 0.21875, ((0, 32), (2, 16)))
    return dict(tokens=tokens, expert_ids=expert_ids, combine=combine, gate_weight=gate_weight, up_weight=up_weight, down_weight=down_weight)


def reference(tokens, expert_ids, combine, gate_weight, up_weight, down_weight):
    count = TOKENS * TOP
    slots = N_EXPERT * CAP
    flat_ids = expert_ids.reshape(-1).astype(jnp.int32)
    flat_weights = combine.reshape(-1)
    order = jnp.argsort(flat_ids, stable=True).astype(jnp.int32)
    sorted_ids = flat_ids[order]
    starts = jnp.searchsorted(sorted_ids, jnp.arange(EXPERTS, dtype=jnp.int32), side="left").astype(jnp.int32)

    def one_expert(total, expert):
        position = starts[expert] + jnp.arange(slots, dtype=jnp.int32)
        clipped = jnp.minimum(position, count - 1).astype(jnp.int32)
        valid = (position < count) & (sorted_ids[clipped] == expert)
        assign = order[clipped]
        owner = (assign // TOP).astype(jnp.int32)
        weight = jnp.where(valid, flat_weights[assign], jnp.float32(0.0))
        rows = tokens[owner]
        gate = jnp.dot(rows, gate_weight[expert], preferred_element_type=jnp.float32)
        up = jnp.dot(rows, up_weight[expert], preferred_element_type=jnp.float32)
        hidden = (jax.nn.silu(gate) * up).astype(jnp.bfloat16)
        output = jnp.dot(hidden, down_weight[expert], preferred_element_type=jnp.float32).astype(jnp.bfloat16)
        total = total.at[owner].add(weight[:, None] * output.astype(jnp.float32))
        return total, None

    start_total = jnp.zeros((TOKENS, D), jnp.float32)
    total, unused = lax.scan(one_expert, start_total, jnp.arange(EXPERTS, dtype=jnp.int32))
    return total.astype(jnp.bfloat16)
```

```python
import functools

import jax
import jax.numpy as jnp
from jax import lax
from jax.experimental import pallas as pl
from jax.experimental.pallas import tpu as pltpu
from jax.sharding import PartitionSpec as P

F32, BF16, F16 = jnp.float32, jnp.bfloat16, jnp.float16
VMEM_LIMIT = 48 * 1024 * 1024


def slot_table(ids, total, capacity):
    rows, top = ids.shape
    lane = lax.broadcasted_iota(jnp.int32, (rows, total), 1)
    named = [ids[:, k : k + 1] == lane for k in range(top)]
    member = functools.reduce(jnp.logical_or, named)
    low = (
        lax.broadcasted_iota(jnp.int32, (rows, rows), 1)
        < lax.broadcasted_iota(jnp.int32, (rows, rows), 0)
    ).astype(F32)
    earlier = jnp.dot(
        low.astype(BF16), member.astype(F32).astype(BF16), preferred_element_type=F32
    )
    place = jnp.where(member, earlier, -1.0).astype(BF16)
    slots = total * capacity
    spread_e = lax.broadcasted_iota(jnp.int32, (total, slots), 0)
    spread_s = lax.broadcasted_iota(jnp.int32, (total, slots), 1)
    first = spread_e * capacity
    spread = ((spread_s >= first) & (spread_s < first + capacity)).astype(F32).astype(BF16)
    place = jnp.dot(place, spread, preferred_element_type=F32)
    offset = (lax.broadcasted_iota(jnp.int32, (1, slots), 1) % capacity).astype(F32)
    return place == offset, spread, named


def dispatch_kernel(total, capacity, ids_ref, tokens_ref, out_ref):
    taken, _, _ = slot_table(ids_ref[...], total, capacity)
    out_ref[...] = lax.dot_general(
        taken.astype(F32).astype(BF16),
        tokens_ref[...],
        (((0,), (0,)), ((), ())),
        preferred_element_type=F32,
    ).astype(BF16)


def weight_kernel(total, capacity, ids_ref, combine_ref, high_ref, low_ref):
    taken, spread, named = slot_table(ids_ref[...], total, capacity)
    combine = combine_ref[...]
    weight = functools.reduce(
        jnp.add, [jnp.where(n, combine[:, k : k + 1], 0.0) for k, n in enumerate(named)]
    )
    high = weight.astype(BF16)
    low = (weight - high.astype(F32)).astype(BF16)
    for part, ref in ((high, high_ref), (low, low_ref)):
        wide = jnp.dot(part, spread, preferred_element_type=F32)
        ref[...] = jnp.where(taken, wide, 0.0).astype(BF16)


def mix_kernel(high_ref, low_ref, back_ref, out_ref):
    back = back_ref[...]
    out_ref[...] = (
        jnp.dot(high_ref[...], back, preferred_element_type=F32)
        + jnp.dot(low_ref[...], back, preferred_element_type=F32)
    ).astype(BF16)


def per_device(tokens, expert_ids, combine, gate_weight, up_weight, down_weight):
    n_cols = lax.axis_size("expert")
    rows, width = tokens.shape
    here, _, ff = gate_weight.shape
    capacity = rows * 5 // 32
    total = n_cols * here
    slots = total * capacity
    params = pltpu.CompilerParams(vmem_limit_bytes=VMEM_LIMIT)
    outgoing = pl.pallas_call(
        functools.partial(dispatch_kernel, total, capacity),
        out_shape=jax.ShapeDtypeStruct((slots, width), BF16),
        compiler_params=params,
    )(expert_ids, tokens)
    high, low = pl.pallas_call(
        functools.partial(weight_kernel, total, capacity),
        out_shape=[jax.ShapeDtypeStruct((rows, slots), BF16)] * 2,
        compiler_params=params,
    )(expert_ids, combine)
    block = here * capacity
    arrived = lax.all_to_all(
        outgoing.reshape(n_cols, block, width), "expert", split_axis=0, concat_axis=0, tiled=True
    ).reshape(slots, width)
    both = jnp.concatenate(
        [gate_weight.reshape(here * width, ff), up_weight.reshape(here * width, ff)], axis=1
    )
    owner = lax.broadcasted_iota(jnp.int32, (slots, 1), 0) % block // capacity

    def by_expert(x):
        return jnp.concatenate(
            [jnp.where(owner == e, x, jnp.zeros((), x.dtype)) for e in range(here)], axis=1
        )

    part = jnp.dot(by_expert(arrived), both, preferred_element_type=F32)
    total_sum = lax.psum((part * 16.0).astype(F16), "dp").astype(F32) * (1.0 / 16.0)
    hidden = (jax.nn.silu(total_sum[:, :ff]) * total_sum[:, ff:]).astype(BF16)
    result = jnp.dot(
        by_expert(hidden), down_weight.reshape(here * ff, width), preferred_element_type=F32
    ).astype(BF16)
    returned = lax.all_to_all(
        result.reshape(n_cols, block, width), "expert", split_axis=0, concat_axis=0, tiled=True
    ).reshape(slots, width)
    return pl.pallas_call(
        mix_kernel,
        out_shape=jax.ShapeDtypeStruct((rows, width), BF16),
        compiler_params=params,
    )(high, low, returned)


def solution(mesh):
    placed = (
        P("expert", "dp"),
        P("expert", None),
        P("expert", None),
        P("expert", "dp", None),
        P("expert", "dp", None),
        P("expert", None, "dp"),
    )
    return jax.shard_map(
        per_device, mesh=mesh, in_specs=placed, out_specs=P("expert", "dp"), check_vma=False
    )
```

```python
import functools

import jax
import jax.numpy as jnp
from jax import lax
from jax.experimental import pallas as pl
from jax.experimental.pallas import tpu as pltpu
from jax.sharding import PartitionSpec as P

F32, BF16, F16 = jnp.float32, jnp.bfloat16, jnp.float16
VMEM_LIMIT = 48 * 1024 * 1024


def slot_table(ids_t, total, capacity):
    top, rows = ids_t.shape
    expert = lax.broadcasted_iota(jnp.int32, (total, rows), 0)
    named = [ids_t[k : k + 1, :] == expert for k in range(top)]
    member = functools.reduce(jnp.logical_or, named)
    before = (
        lax.broadcasted_iota(jnp.int32, (rows, rows), 0)
        < lax.broadcasted_iota(jnp.int32, (rows, rows), 1)
    ).astype(F32)
    earlier = jnp.dot(
        member.astype(F32).astype(BF16), before.astype(BF16), preferred_element_type=F32
    )
    place = jnp.where(member, earlier, -1.0).astype(BF16)
    slots = total * capacity
    first = lax.broadcasted_iota(jnp.int32, (slots, total), 1) * capacity
    slot = lax.broadcasted_iota(jnp.int32, (slots, total), 0)
    spread = ((slot >= first) & (slot < first + capacity)).astype(F32).astype(BF16)
    place = jnp.dot(spread, place, preferred_element_type=F32)
    slot = lax.broadcasted_iota(jnp.int32, (slots, rows), 0).astype(F32)
    offset = slot - capacity * jnp.floor((slot + 0.5) * (1.0 / capacity))
    return place == offset, spread, named


def dispatch_kernel(total, capacity, ids_ref, tokens_ref, out_ref, held, sem):
    copy = pltpu.make_async_copy(tokens_ref, held, sem)
    copy.start()
    taken, _, _ = slot_table(ids_ref[...], total, capacity)
    taken = taken.astype(F32).astype(BF16)
    copy.wait()
    out_ref[...] = jnp.dot(taken, held[...], preferred_element_type=F32).astype(BF16)


def weight_kernel(total, capacity, ids_ref, combine_ref, high_ref, low_ref):
    taken, spread, named = slot_table(ids_ref[...], total, capacity)
    combine = combine_ref[...]
    weight = functools.reduce(
        jnp.add, [jnp.where(n, combine[k : k + 1, :], 0.0) for k, n in enumerate(named)]
    )
    high = weight.astype(BF16)
    low = (weight - high.astype(F32)).astype(BF16)
    for part, ref in ((high, high_ref), (low, low_ref)):
        wide = jnp.dot(spread, part, preferred_element_type=F32)
        ref[...] = jnp.where(taken, wide, 0.0).T.astype(BF16)


def down_kernel(capacity, hidden_ref, down_ref, out_ref):
    hidden = hidden_ref[...]
    here = down_ref.shape[0]
    row = lax.broadcasted_iota(jnp.int32, out_ref.shape, 0).astype(F32)
    block = here * capacity
    row = row - block * jnp.floor((row + 0.5) * (1.0 / block))
    out = jnp.dot(hidden, down_ref[0], preferred_element_type=F32)
    for e in range(1, here):
        other = jnp.dot(hidden, down_ref[e], preferred_element_type=F32)
        out = jnp.where(row < e * capacity, out, other)
    out_ref[...] = out.astype(BF16)


def mix_kernel(high_ref, low_ref, back_ref, out_ref):
    back = back_ref[...]
    out_ref[...] = (
        jnp.dot(high_ref[...], back, preferred_element_type=F32)
        + jnp.dot(low_ref[...], back, preferred_element_type=F32)
    ).astype(BF16)


def per_device(tokens, expert_ids, combine, gate_weight, up_weight, down_weight):
    n_cols = lax.axis_size("expert")
    rows, width = tokens.shape
    here, _, ff = gate_weight.shape
    capacity = rows * 5 // 32
    total = n_cols * here
    slots = total * capacity
    ids_t = expert_ids.T
    params = pltpu.CompilerParams(vmem_limit_bytes=VMEM_LIMIT)
    outgoing = pl.pallas_call(
        functools.partial(dispatch_kernel, total, capacity),
        out_shape=jax.ShapeDtypeStruct((slots, width), BF16),
        in_specs=[pl.BlockSpec(memory_space=pltpu.VMEM), pl.BlockSpec(memory_space=pl.ANY)],
        scratch_shapes=[pltpu.VMEM((rows, width), BF16), pltpu.SemaphoreType.DMA],
        compiler_params=params,
    )(ids_t, tokens)
    high, low = pl.pallas_call(
        functools.partial(weight_kernel, total, capacity),
        out_shape=[jax.ShapeDtypeStruct((rows, slots), BF16)] * 2,
        compiler_params=params,
    )(ids_t, combine.T)
    block = here * capacity
    arrived = lax.all_to_all(
        outgoing.reshape(n_cols, block, width), "expert", split_axis=0, concat_axis=0, tiled=True
    ).reshape(slots, width)
    both = jnp.concatenate(
        [gate_weight.reshape(here * width, ff), up_weight.reshape(here * width, ff)], axis=1
    )
    owner = lax.broadcasted_iota(jnp.int32, (slots, 1), 0) % block // capacity

    def by_expert(x):
        return jnp.concatenate(
            [jnp.where(owner == e, x, jnp.zeros((), x.dtype)) for e in range(here)], axis=1
        )

    part = jnp.dot(by_expert(arrived), both, preferred_element_type=F32)
    sums = lax.psum((part * 16.0).astype(F16), "dp")
    gate = sums[:, :ff].astype(F32) * (1.0 / 16.0)
    up = sums[:, ff:].astype(F32) * (1.0 / 16.0)
    hidden = (jax.nn.silu(gate) * up).astype(BF16)
    result = pl.pallas_call(
        functools.partial(down_kernel, capacity),
        out_shape=jax.ShapeDtypeStruct((slots, width), BF16),
        compiler_params=params,
    )(hidden, down_weight)
    returned = lax.all_to_all(
        result.reshape(n_cols, block, width), "expert", split_axis=0, concat_axis=0, tiled=True
    ).reshape(slots, width)
    return pl.pallas_call(
        mix_kernel,
        out_shape=jax.ShapeDtypeStruct((rows, width), BF16),
        compiler_params=params,
    )(high, low, returned)


def solution(mesh):
    placed = (
        P("expert", "dp"),
        P("expert", None),
        P("expert", None),
        P("expert", "dp", None),
        P("expert", "dp", None),
        P("expert", None, "dp"),
    )
    return jax.shard_map(
        per_device, mesh=mesh, in_specs=placed, out_specs=P("expert", "dp"), check_vma=False
    )
```

```python
import functools

import jax
import jax.numpy as jnp
from jax import lax
from jax.experimental import pallas as pl
from jax.experimental.pallas import tpu as pltpu
from jax.sharding import PartitionSpec as P

F32, BF16, F16 = jnp.float32, jnp.bfloat16, jnp.float16
VMEM_LIMIT = 48 * 1024 * 1024


def slot_table(ids_t, total, capacity):
    top, rows = ids_t.shape
    expert = lax.broadcasted_iota(jnp.int32, (total, rows), 0)
    named = [ids_t[k : k + 1, :] == expert for k in range(top)]
    member = functools.reduce(jnp.logical_or, named)
    before = (
        lax.broadcasted_iota(jnp.int32, (rows, rows), 0)
        < lax.broadcasted_iota(jnp.int32, (rows, rows), 1)
    ).astype(F32)
    earlier = jnp.dot(
        member.astype(F32).astype(BF16), before.astype(BF16), preferred_element_type=F32
    )
    place = jnp.where(member, earlier, -1.0).astype(BF16)
    slots = total * capacity
    first = lax.broadcasted_iota(jnp.int32, (slots, total), 1) * capacity
    slot = lax.broadcasted_iota(jnp.int32, (slots, total), 0)
    spread = ((slot >= first) & (slot < first + capacity)).astype(F32).astype(BF16)
    place = jnp.dot(spread, place, preferred_element_type=F32)
    slot = lax.broadcasted_iota(jnp.int32, (slots, rows), 0).astype(F32)
    offset = slot - capacity * jnp.floor((slot + 0.5) * (1.0 / capacity))
    return place == offset, spread, named


def dispatch_kernel(total, capacity, ids_ref, tokens_ref, out_ref, ids, tokens, sems):
    fetch_ids = pltpu.make_async_copy(ids_ref, ids, sems.at[0])
    fetch_tokens = pltpu.make_async_copy(tokens_ref, tokens, sems.at[1])
    fetch_ids.start()
    fetch_tokens.start()
    fetch_ids.wait()
    taken, _, _ = slot_table(ids[...], total, capacity)
    taken = taken.astype(F32).astype(BF16)
    fetch_tokens.wait()
    out_ref[...] = jnp.dot(taken, tokens[...], preferred_element_type=F32).astype(BF16)


def weight_kernel(total, capacity, ids_ref, combine_ref, high_ref, low_ref):
    taken, spread, named = slot_table(ids_ref[...], total, capacity)
    combine = combine_ref[...]
    weight = functools.reduce(
        jnp.add, [jnp.where(n, combine[k : k + 1, :], 0.0) for k, n in enumerate(named)]
    )
    high = weight.astype(BF16)
    low = (weight - high.astype(F32)).astype(BF16)
    for part, ref in ((high, high_ref), (low, low_ref)):
        wide = jnp.dot(spread, part, preferred_element_type=F32)
        ref[...] = jnp.where(taken, wide, 0.0).T.astype(BF16)


def down_kernel(capacity, hidden_ref, down_ref, out_ref):
    hidden = hidden_ref[...]
    here = down_ref.shape[0]
    row = lax.broadcasted_iota(jnp.int32, out_ref.shape, 0).astype(F32)
    block = here * capacity
    row = row - block * jnp.floor((row + 0.5) * (1.0 / block))
    out = jnp.dot(hidden, down_ref[0], preferred_element_type=F32)
    for e in range(1, here):
        other = jnp.dot(hidden, down_ref[e], preferred_element_type=F32)
        out = jnp.where(row < e * capacity, out, other)
    out_ref[...] = out.astype(BF16)


def mix_kernel(high_ref, low_ref, back_ref, out_ref):
    back = back_ref[...]
    out_ref[...] = (
        jnp.dot(high_ref[...], back, preferred_element_type=F32)
        + jnp.dot(low_ref[...], back, preferred_element_type=F32)
    ).astype(BF16)


def per_device(tokens, expert_ids, combine, gate_weight, up_weight, down_weight):
    n_cols = lax.axis_size("expert")
    rows, width = tokens.shape
    here, _, ff = gate_weight.shape
    capacity = rows * 5 // 32
    total = n_cols * here
    slots = total * capacity
    ids_t = expert_ids.T
    params = pltpu.CompilerParams(vmem_limit_bytes=VMEM_LIMIT)
    outgoing = pl.pallas_call(
        functools.partial(dispatch_kernel, total, capacity),
        out_shape=jax.ShapeDtypeStruct((slots, width), BF16),
        in_specs=[pl.BlockSpec(memory_space=pltpu.HBM)] * 2,
        scratch_shapes=[
            pltpu.VMEM(ids_t.shape, jnp.int32),
            pltpu.VMEM((rows, width), BF16),
            pltpu.SemaphoreType.DMA((2,)),
        ],
    )(ids_t, tokens)
    high, low = pl.pallas_call(
        functools.partial(weight_kernel, total, capacity),
        out_shape=[jax.ShapeDtypeStruct((rows, slots), BF16)] * 2,
        compiler_params=params,
    )(ids_t, combine.T)
    block = here * capacity
    arrived = lax.all_to_all(
        outgoing.reshape(n_cols, block, width), "expert", split_axis=0, concat_axis=0, tiled=True
    ).reshape(slots, width)
    owner = lax.broadcasted_iota(jnp.int32, (slots, 1), 0) % block // capacity

    def by_expert(x):
        return jnp.concatenate(
            [jnp.where(owner == e, x, jnp.zeros((), x.dtype)) for e in range(here)], axis=1
        )

    rows_in = by_expert(arrived)

    def project(weight):
        part = jnp.dot(rows_in, weight.reshape(here * width, ff), preferred_element_type=F32)
        return (part * 16.0).astype(F16)

    gate, up = lax.psum((project(gate_weight), project(up_weight)), "dp")
    gate, up = gate.astype(F32) * (1.0 / 16.0), up.astype(F32) * (1.0 / 16.0)
    hidden = (jax.nn.silu(gate) * up).astype(BF16)
    result = pl.pallas_call(
        functools.partial(down_kernel, capacity),
        out_shape=jax.ShapeDtypeStruct((slots, width), BF16),
        compiler_params=params,
    )(hidden, down_weight)
    returned = lax.all_to_all(
        result.reshape(n_cols, block, width), "expert", split_axis=0, concat_axis=0, tiled=True
    ).reshape(slots, width)
    return pl.pallas_call(
        mix_kernel,
        out_shape=jax.ShapeDtypeStruct((rows, width), BF16),
        compiler_params=params,
    )(high, low, returned)


def solution(mesh):
    placed = (
        P("expert", "dp"),
        P("expert", None),
        P("expert", None),
        P("expert", "dp", None),
        P("expert", "dp", None),
        P("expert", None, "dp"),
    )
    return jax.shard_map(
        per_device, mesh=mesh, in_specs=placed, out_specs=P("expert", "dp"), check_vma=False
    )
```

```python
import functools

import jax
import jax.numpy as jnp
from jax import lax
from jax.experimental import pallas as pl
from jax.experimental.pallas import tpu as pltpu
from jax.sharding import PartitionSpec as P

F32, BF16, F16 = jnp.float32, jnp.bfloat16, jnp.float16
VMEM_LIMIT = 48 * 1024 * 1024


def slot_owner(total, capacity):
    slots = total * capacity
    first = lax.broadcasted_iota(jnp.int32, (slots, total), 1) * capacity
    slot = lax.broadcasted_iota(jnp.int32, (slots, total), 0)
    return ((slot >= first) & (slot < first + capacity)).astype(F32).astype(BF16)


def slot_offset(total, capacity, rows):
    slot = lax.broadcasted_iota(jnp.int32, (total * capacity, rows), 0).astype(F32)
    return slot - capacity * jnp.floor((slot + 0.5) * (1.0 / capacity))


def earlier_tokens(rows):
    earlier = lax.broadcasted_iota(jnp.int32, (rows, rows), 0)
    return (earlier < lax.broadcasted_iota(jnp.int32, (rows, rows), 1)).astype(F32).astype(BF16)


def places(ids_t, total, earlier):
    top, rows = ids_t.shape
    expert = lax.broadcasted_iota(jnp.int32, (total, rows), 0)
    named = [ids_t[k : k + 1, :] == expert for k in range(top)]
    member = functools.reduce(jnp.logical_or, named)
    count = jnp.dot(member.astype(F32).astype(BF16), earlier, preferred_element_type=F32)
    return jnp.where(member, count, -1.0).astype(BF16), named


def dispatch_kernel(total, capacity, ids_ref, tokens_ref, out_ref, ids, tokens, chunks, sems):
    parts, part = chunks.shape[0], chunks.shape[1]
    rows = tokens.shape[0]
    fetch_ids = pltpu.make_async_copy(ids_ref, ids, sems.at[0])
    fetch_tokens = pltpu.make_async_copy(tokens_ref, tokens, sems.at[1])
    fetch_ids.start()
    fetch_tokens.start()
    owner = slot_owner(total, capacity)
    offset = slot_offset(total, capacity, rows)
    earlier = earlier_tokens(rows)
    fetch_ids.wait()
    place, _ = places(ids[...], total, earlier)
    fetch_tokens.wait()
    held = tokens[...]
    sends = []
    for i in range(parts):
        own = slice(i * part, (i + 1) * part)
        wide = jnp.dot(owner[own], place, preferred_element_type=F32)
        taken = (wide == offset[own]).astype(F32).astype(BF16)
        chunks[i] = jnp.dot(taken, held, preferred_element_type=F32).astype(BF16)
        send = pltpu.make_async_copy(
            chunks.at[i], out_ref.at[pl.ds(i * part, part)], sems.at[2 + i]
        )
        send.start()
        sends.append(send)
    for send in sends:
        send.wait()


def weight_kernel(total, capacity, ids_ref, combine_ref, high_ref, low_ref):
    spread = slot_owner(total, capacity)
    place, named = places(ids_ref[...], total, earlier_tokens(ids_ref.shape[1]))
    wide = jnp.dot(spread, place, preferred_element_type=F32)
    taken = wide == slot_offset(total, capacity, ids_ref.shape[1])
    combine = combine_ref[...]
    weight = functools.reduce(
        jnp.add, [jnp.where(n, combine[k : k + 1, :], 0.0) for k, n in enumerate(named)]
    )
    high = weight.astype(BF16)
    low = (weight - high.astype(F32)).astype(BF16)
    for part, ref in ((high, high_ref), (low, low_ref)):
        wide = jnp.dot(spread, part, preferred_element_type=F32)
        ref[...] = jnp.where(taken, wide, 0.0).T.astype(BF16)


def down_kernel(capacity, hidden_ref, down_ref, out_ref, chunks, sems):
    here = down_ref.shape[0]
    parts, part, width = chunks.shape
    block = here * capacity
    row = lax.broadcasted_iota(jnp.int32, (part, width), 0).astype(F32)
    row = row - block * jnp.floor((row + 0.5) * (1.0 / block))
    sends = []
    for i in range(parts):
        hidden = hidden_ref[i * part : (i + 1) * part]
        out = jnp.dot(hidden, down_ref[0], preferred_element_type=F32)
        for e in range(1, here):
            other = jnp.dot(hidden, down_ref[e], preferred_element_type=F32)
            out = jnp.where(row < e * capacity, out, other)
        chunks[i] = out.astype(BF16)
        send = pltpu.make_async_copy(
            chunks.at[i], out_ref.at[pl.ds(i * part, part)], sems.at[i]
        )
        send.start()
        sends.append(send)
    for send in sends:
        send.wait()


def split_kernel(capacity, rows_ref, out_ref):
    here, width = out_ref.shape[1] // rows_ref.shape[1], rows_ref.shape[1]
    block = here * capacity
    row = lax.broadcasted_iota(jnp.int32, rows_ref.shape, 0).astype(F32)
    row = row - block * jnp.floor((row + 0.5) * (1.0 / block))
    rows = rows_ref[...]
    for e in range(here):
        own = (row >= e * capacity) & (row < (e + 1) * capacity)
        out_ref[:, e * width : (e + 1) * width] = jnp.where(own, rows, jnp.zeros((), BF16))


def mix_kernel(high_ref, low_ref, back_ref, out_ref):
    back = back_ref[...]
    out_ref[...] = (
        jnp.dot(high_ref[...], back, preferred_element_type=F32)
        + jnp.dot(low_ref[...], back, preferred_element_type=F32)
    ).astype(BF16)


def per_device(tokens, expert_ids, combine, gate_weight, up_weight, down_weight):
    n_cols = lax.axis_size("expert")
    rows, width = tokens.shape
    here, _, ff = gate_weight.shape
    capacity = rows * 5 // 32
    total = n_cols * here
    slots = total * capacity
    parts = 5
    ids_t = expert_ids.T
    params = pltpu.CompilerParams(vmem_limit_bytes=VMEM_LIMIT)
    outgoing = pl.pallas_call(
        functools.partial(dispatch_kernel, total, capacity),
        out_shape=jax.ShapeDtypeStruct((slots, width), BF16),
        in_specs=[pl.BlockSpec(memory_space=pltpu.HBM)] * 2,
        out_specs=pl.BlockSpec(memory_space=pltpu.HBM),
        scratch_shapes=[
            pltpu.VMEM(ids_t.shape, jnp.int32),
            pltpu.VMEM((rows, width), BF16),
            pltpu.VMEM((parts, slots // parts, width), BF16),
            pltpu.SemaphoreType.DMA((2 + parts,)),
        ],
    )(ids_t, tokens)
    high, low = pl.pallas_call(
        functools.partial(weight_kernel, total, capacity),
        out_shape=[jax.ShapeDtypeStruct((rows, slots), BF16)] * 2,
        compiler_params=params,
    )(ids_t, combine.T)
    block = here * capacity
    arrived = lax.all_to_all(
        outgoing.reshape(n_cols, block, width), "expert", split_axis=0, concat_axis=0, tiled=True
    ).reshape(slots, width)
    rows_in = pl.pallas_call(
        functools.partial(split_kernel, capacity),
        out_shape=jax.ShapeDtypeStruct((slots, here * width), BF16),
        compiler_params=params,
    )(arrived)

    def project(weight):
        part = jnp.dot(rows_in, weight.reshape(here * width, ff), preferred_element_type=F32)
        return (part * 16.0).astype(F16)

    gate, up = lax.psum((project(gate_weight), project(up_weight)), "dp")
    gate, up = gate.astype(F32) * (1.0 / 16.0), up.astype(F32) * (1.0 / 16.0)
    hidden = (jax.nn.silu(gate) * up).astype(BF16)
    result = pl.pallas_call(
        functools.partial(down_kernel, capacity),
        out_shape=jax.ShapeDtypeStruct((slots, width), BF16),
        in_specs=[pl.BlockSpec(memory_space=pltpu.VMEM)] * 2,
        out_specs=pl.BlockSpec(memory_space=pltpu.HBM),
        scratch_shapes=[
            pltpu.VMEM((4, slots // 4, width), BF16),
            pltpu.SemaphoreType.DMA((4,)),
        ],
        compiler_params=params,
    )(hidden, down_weight)
    returned = lax.all_to_all(
        result.reshape(n_cols, block, width), "expert", split_axis=0, concat_axis=0, tiled=True
    ).reshape(slots, width)
    return pl.pallas_call(
        mix_kernel,
        out_shape=jax.ShapeDtypeStruct((rows, width), BF16),
        compiler_params=params,
    )(high, low, returned)


def solution(mesh):
    placed = (
        P("expert", "dp"),
        P("expert", None),
        P("expert", None),
        P("expert", "dp", None),
        P("expert", "dp", None),
        P("expert", None, "dp"),
    )
    return jax.shard_map(
        per_device, mesh=mesh, in_specs=placed, out_specs=P("expert", "dp"), check_vma=False
    )
```

```python
import functools

import jax
import jax.numpy as jnp
from jax import lax
from jax.experimental import pallas as pl
from jax.experimental.pallas import tpu as pltpu
from jax.sharding import PartitionSpec as P

F32, BF16, F16 = jnp.float32, jnp.bfloat16, jnp.float16
VMEM_LIMIT = 48 * 1024 * 1024


def slot_owner(total, capacity):
    slots = total * capacity
    first = lax.broadcasted_iota(jnp.int32, (slots, total), 1) * capacity
    slot = lax.broadcasted_iota(jnp.int32, (slots, total), 0)
    return ((slot >= first) & (slot < first + capacity)).astype(F32).astype(BF16)


def slot_offset(total, capacity, rows):
    slot = lax.broadcasted_iota(jnp.int32, (total * capacity, rows), 0).astype(F32)
    return slot - capacity * jnp.floor((slot + 0.5) * (1.0 / capacity))


def earlier_tokens(rows):
    earlier = lax.broadcasted_iota(jnp.int32, (rows, rows), 0)
    return (earlier < lax.broadcasted_iota(jnp.int32, (rows, rows), 1)).astype(F32).astype(BF16)


def places(ids_t, total, earlier):
    top, rows = ids_t.shape
    expert = lax.broadcasted_iota(jnp.int32, (total, rows), 0)
    named = [ids_t[k : k + 1, :] == expert for k in range(top)]
    member = functools.reduce(jnp.logical_or, named)
    count = jnp.dot(member.astype(F32).astype(BF16), earlier, preferred_element_type=F32)
    return jnp.where(member, count, -1.0).astype(BF16), named


def dispatch_kernel(total, capacity, ids_ref, tokens_ref, out_ref, ids, tokens, chunks, sems):
    parts, part = chunks.shape[0], chunks.shape[1]
    rows = tokens.shape[0]
    fetch_ids = pltpu.make_async_copy(ids_ref, ids, sems.at[0])
    fetch_tokens = pltpu.make_async_copy(tokens_ref, tokens, sems.at[1])
    fetch_ids.start()
    fetch_tokens.start()
    owner = slot_owner(total, capacity)
    offset = slot_offset(total, capacity, rows)
    earlier = earlier_tokens(rows)
    fetch_ids.wait()
    place, _ = places(ids[...], total, earlier)
    fetch_tokens.wait()
    held = tokens[...]
    sends = []
    for i in range(parts):
        own = slice(i * part, (i + 1) * part)
        wide = jnp.dot(owner[own], place, preferred_element_type=F32)
        taken = (wide == offset[own]).astype(F32).astype(BF16)
        chunks[i] = jnp.dot(taken, held, preferred_element_type=F32).astype(BF16)
        send = pltpu.make_async_copy(
            chunks.at[i], out_ref.at[pl.ds(i * part, part)], sems.at[2 + i]
        )
        send.start()
        sends.append(send)
    for send in sends:
        send.wait()


def weight_kernel(total, capacity, ids_ref, combine_ref, high_ref, low_ref):
    spread = slot_owner(total, capacity)
    place, named = places(ids_ref[...], total, earlier_tokens(ids_ref.shape[1]))
    wide = jnp.dot(spread, place, preferred_element_type=F32)
    taken = wide == slot_offset(total, capacity, ids_ref.shape[1])
    combine = combine_ref[...]
    weight = functools.reduce(
        jnp.add, [jnp.where(n, combine[k : k + 1, :], 0.0) for k, n in enumerate(named)]
    )
    high = weight.astype(BF16)
    low = (weight - high.astype(F32)).astype(BF16)
    for part, ref in ((high, high_ref), (low, low_ref)):
        wide = jnp.dot(spread, part, preferred_element_type=F32)
        ref[...] = jnp.where(taken, wide, 0.0).T.astype(BF16)


def select_kernel(capacity, outs_ref, out_ref):
    width = out_ref.shape[1]
    here = outs_ref.shape[1] // width
    block = here * capacity
    row = lax.broadcasted_iota(jnp.int32, out_ref.shape, 0).astype(F32)
    row = row - block * jnp.floor((row + 0.5) * (1.0 / block))
    out = outs_ref[:, :width]
    for e in range(1, here):
        out = jnp.where(row < e * capacity, out, outs_ref[:, e * width : (e + 1) * width])
    out_ref[...] = out


def split_kernel(capacity, rows_ref, out_ref):
    here, width = out_ref.shape[1] // rows_ref.shape[1], rows_ref.shape[1]
    block = here * capacity
    row = lax.broadcasted_iota(jnp.int32, rows_ref.shape, 0).astype(F32)
    row = row - block * jnp.floor((row + 0.5) * (1.0 / block))
    rows = rows_ref[...]
    for e in range(here):
        own = (row >= e * capacity) & (row < (e + 1) * capacity)
        out_ref[:, e * width : (e + 1) * width] = jnp.where(own, rows, jnp.zeros((), BF16))


def mix_kernel(high_ref, low_ref, back_ref, out_ref):
    back = back_ref[...]
    out_ref[...] = (
        jnp.dot(high_ref[...], back, preferred_element_type=F32)
        + jnp.dot(low_ref[...], back, preferred_element_type=F32)
    ).astype(BF16)


def per_device(tokens, expert_ids, combine, gate_weight, up_weight, down_weight):
    n_cols = lax.axis_size("expert")
    rows, width = tokens.shape
    here, _, ff = gate_weight.shape
    capacity = rows * 5 // 32
    total = n_cols * here
    slots = total * capacity
    parts = 5
    ids_t = expert_ids.T
    params = pltpu.CompilerParams(vmem_limit_bytes=VMEM_LIMIT)
    outgoing = pl.pallas_call(
        functools.partial(dispatch_kernel, total, capacity),
        out_shape=jax.ShapeDtypeStruct((slots, width), BF16),
        in_specs=[pl.BlockSpec(memory_space=pltpu.HBM)] * 2,
        out_specs=pl.BlockSpec(memory_space=pltpu.HBM),
        scratch_shapes=[
            pltpu.VMEM(ids_t.shape, jnp.int32),
            pltpu.VMEM((rows, width), BF16),
            pltpu.VMEM((parts, slots // parts, width), BF16),
            pltpu.SemaphoreType.DMA((2 + parts,)),
        ],
    )(ids_t, tokens)
    high, low = pl.pallas_call(
        functools.partial(weight_kernel, total, capacity),
        out_shape=[jax.ShapeDtypeStruct((rows, slots), BF16)] * 2,
        compiler_params=params,
    )(ids_t, combine.T)
    block = here * capacity
    arrived = lax.all_to_all(
        outgoing.reshape(n_cols, block, width), "expert", split_axis=0, concat_axis=0, tiled=True
    ).reshape(slots, width)
    rows_in = pl.pallas_call(
        functools.partial(split_kernel, capacity),
        out_shape=jax.ShapeDtypeStruct((slots, here * width), BF16),
        compiler_params=params,
    )(arrived)

    def project(weight):
        part = jnp.dot(rows_in, weight.reshape(here * width, ff), preferred_element_type=F32)
        return (part * 16.0).astype(F16)

    gate, up = lax.psum((project(gate_weight), project(up_weight)), "dp")
    gate, up = gate.astype(F32) * (1.0 / 16.0), up.astype(F32) * (1.0 / 16.0)
    hidden = (jax.nn.silu(gate) * up).astype(BF16)
    both = jnp.concatenate([down_weight[e] for e in range(here)], axis=1)
    outs = jnp.dot(hidden, both, preferred_element_type=F32).astype(BF16)
    result = pl.pallas_call(
        functools.partial(select_kernel, capacity),
        out_shape=jax.ShapeDtypeStruct((slots, width), BF16),
        compiler_params=params,
    )(outs)
    result, high, low = lax.optimization_barrier((result, high, low))
    returned = lax.all_to_all(
        result.reshape(n_cols, block, width), "expert", split_axis=0, concat_axis=0, tiled=True
    ).reshape(slots, width)
    return pl.pallas_call(
        mix_kernel,
        out_shape=jax.ShapeDtypeStruct((rows, width), BF16),
        compiler_params=params,
    )(high, low, returned)


def solution(mesh):
    placed = (
        P("expert", "dp"),
        P("expert", None),
        P("expert", None),
        P("expert", "dp", None),
        P("expert", "dp", None),
        P("expert", None, "dp"),
    )
    return jax.shard_map(
        per_device, mesh=mesh, in_specs=placed, out_specs=P("expert", "dp"), check_vma=False
    )
```

```python
import functools

import jax
import jax.numpy as jnp
from jax import lax
from jax.experimental import pallas as pl
from jax.experimental.pallas import tpu as pltpu
from jax.sharding import PartitionSpec as P

F32, BF16, F16 = jnp.float32, jnp.bfloat16, jnp.float16
VMEM_LIMIT = 48 * 1024 * 1024


def slot_owner(total, capacity):
    slots = total * capacity
    first = lax.broadcasted_iota(jnp.int32, (slots, total), 1) * capacity
    slot = lax.broadcasted_iota(jnp.int32, (slots, total), 0)
    return ((slot >= first) & (slot < first + capacity)).astype(F32).astype(BF16)


def slot_offset(total, capacity, rows):
    slot = lax.broadcasted_iota(jnp.int32, (total * capacity, rows), 0).astype(F32)
    return slot - capacity * jnp.floor((slot + 0.5) * (1.0 / capacity))


def earlier_tokens(rows):
    earlier = lax.broadcasted_iota(jnp.int32, (rows, rows), 0)
    return (earlier < lax.broadcasted_iota(jnp.int32, (rows, rows), 1)).astype(F32).astype(BF16)


def places(ids_t, total, earlier):
    top, rows = ids_t.shape
    expert = lax.broadcasted_iota(jnp.int32, (total, rows), 0)
    named = [ids_t[k : k + 1, :] == expert for k in range(top)]
    member = functools.reduce(jnp.logical_or, named)
    count = jnp.dot(member.astype(F32).astype(BF16), earlier, preferred_element_type=F32)
    return jnp.where(member, count, -1.0).astype(BF16), named


def dispatch_kernel(total, capacity, ids_ref, tokens_ref, out_ref, ids, tokens, chunks, sems):
    parts, part = chunks.shape[0], chunks.shape[1]
    rows = tokens.shape[0]
    fetch_ids = pltpu.make_async_copy(ids_ref, ids, sems.at[0])
    fetch_tokens = pltpu.make_async_copy(tokens_ref, tokens, sems.at[1])
    fetch_ids.start()
    fetch_tokens.start()
    owner = slot_owner(total, capacity)
    offset = slot_offset(total, capacity, rows)
    earlier = earlier_tokens(rows)
    fetch_ids.wait()
    place, _ = places(ids[...], total, earlier)
    fetch_tokens.wait()
    held = tokens[...]
    sends = []
    for i in range(parts):
        own = slice(i * part, (i + 1) * part)
        wide = jnp.dot(owner[own], place, preferred_element_type=F32)
        taken = (wide == offset[own]).astype(F32).astype(BF16)
        chunks[i] = jnp.dot(taken, held, preferred_element_type=F32).astype(BF16)
        send = pltpu.make_async_copy(
            chunks.at[i], out_ref.at[pl.ds(i * part, part)], sems.at[2 + i]
        )
        send.start()
        sends.append(send)
    for send in sends:
        send.wait()


def weight_kernel(total, capacity, ids_ref, combine_ref, high_ref, low_ref):
    spread = slot_owner(total, capacity)
    place, named = places(ids_ref[...], total, earlier_tokens(ids_ref.shape[1]))
    wide = jnp.dot(spread, place, preferred_element_type=F32)
    taken = wide == slot_offset(total, capacity, ids_ref.shape[1])
    combine = combine_ref[...]
    weight = functools.reduce(
        jnp.add, [jnp.where(n, combine[k : k + 1, :], 0.0) for k, n in enumerate(named)]
    )
    high = weight.astype(BF16)
    low = (weight - high.astype(F32)).astype(BF16)
    for part, ref in ((high, high_ref), (low, low_ref)):
        wide = jnp.dot(spread, part, preferred_element_type=F32)
        ref[...] = jnp.where(taken, wide, 0.0).T.astype(BF16)


def select_kernel(capacity, outs_ref, out_ref):
    width = out_ref.shape[1]
    here = outs_ref.shape[1] // width
    block = here * capacity
    row = lax.broadcasted_iota(jnp.int32, out_ref.shape, 0).astype(F32)
    row = row - block * jnp.floor((row + 0.5) * (1.0 / block))
    out = outs_ref[:, :width]
    for e in range(1, here):
        out = jnp.where(row < e * capacity, out, outs_ref[:, e * width : (e + 1) * width])
    out_ref[...] = out


def split_kernel(capacity, rows_ref, out_ref):
    here, width = out_ref.shape[1] // rows_ref.shape[1], rows_ref.shape[1]
    block = here * capacity
    row = lax.broadcasted_iota(jnp.int32, rows_ref.shape, 0).astype(F32)
    row = row - block * jnp.floor((row + 0.5) * (1.0 / block))
    rows = rows_ref[...]
    for e in range(here):
        own = (row >= e * capacity) & (row < (e + 1) * capacity)
        out_ref[:, e * width : (e + 1) * width] = jnp.where(own, rows, jnp.zeros((), BF16))


def mix_kernel(high_ref, low_ref, back_ref, out_ref):
    back = back_ref[...]
    out_ref[...] = (
        jnp.dot(high_ref[...], back, preferred_element_type=F32)
        + jnp.dot(low_ref[...], back, preferred_element_type=F32)
    ).astype(BF16)


def per_device(tokens, expert_ids, combine, gate_weight, up_weight, down_weight):
    n_cols = lax.axis_size("expert")
    rows, width = tokens.shape
    here, _, ff = gate_weight.shape
    capacity = rows * 5 // 32
    total = n_cols * here
    slots = total * capacity
    parts = 2
    ids_t = expert_ids.T
    params = pltpu.CompilerParams(vmem_limit_bytes=VMEM_LIMIT)
    outgoing = pl.pallas_call(
        functools.partial(dispatch_kernel, total, capacity),
        out_shape=jax.ShapeDtypeStruct((slots, width), BF16),
        in_specs=[pl.BlockSpec(memory_space=pltpu.HBM)] * 2,
        out_specs=pl.BlockSpec(memory_space=pltpu.HBM),
        scratch_shapes=[
            pltpu.VMEM(ids_t.shape, jnp.int32),
            pltpu.VMEM((rows, width), BF16),
            pltpu.VMEM((parts, slots // parts, width), BF16),
            pltpu.SemaphoreType.DMA((2 + parts,)),
        ],
    )(ids_t, tokens)
    high, low = pl.pallas_call(
        functools.partial(weight_kernel, total, capacity),
        out_shape=[jax.ShapeDtypeStruct((rows, slots), BF16)] * 2,
        compiler_params=params,
    )(ids_t, combine.T)
    block = here * capacity
    arrived = lax.all_to_all(
        outgoing.reshape(n_cols, block, width), "expert", split_axis=0, concat_axis=0, tiled=True
    ).reshape(slots, width)
    rows_in = pl.pallas_call(
        functools.partial(split_kernel, capacity),
        out_shape=jax.ShapeDtypeStruct((slots, here * width), BF16),
        compiler_params=params,
    )(arrived)

    def project(weight):
        part = jnp.dot(rows_in, weight.reshape(here * width, ff), preferred_element_type=F32)
        return (part * 16.0).astype(F16)

    gate, up = lax.psum((project(gate_weight), project(up_weight)), "dp")
    gate, up = gate.astype(F32) * (1.0 / 16.0), up.astype(F32) * (1.0 / 16.0)
    hidden = (jax.nn.silu(gate) * up).astype(BF16)
    both = jnp.concatenate([down_weight[e] for e in range(here)], axis=1)
    outs = jnp.dot(hidden, both, preferred_element_type=F32).astype(BF16)
    result = pl.pallas_call(
        functools.partial(select_kernel, capacity),
        out_shape=jax.ShapeDtypeStruct((slots, width), BF16),
        compiler_params=params,
    )(outs)
    result, high, low = lax.optimization_barrier((result, high, low))
    returned = lax.all_to_all(
        result.reshape(n_cols, block, width), "expert", split_axis=0, concat_axis=0, tiled=True
    ).reshape(slots, width)
    return pl.pallas_call(
        mix_kernel,
        out_shape=jax.ShapeDtypeStruct((rows, width), BF16),
        compiler_params=params,
    )(high, low, returned)


def solution(mesh):
    placed = (
        P("expert", "dp"),
        P("expert", None),
        P("expert", None),
        P("expert", "dp", None),
        P("expert", "dp", None),
        P("expert", None, "dp"),
    )
    return jax.shard_map(
        per_device, mesh=mesh, in_specs=placed, out_specs=P("expert", "dp"), check_vma=False
    )
```

```python
import functools

import jax
import jax.numpy as jnp
from jax import lax
from jax.experimental import pallas as pl
from jax.experimental.pallas import tpu as pltpu
from jax.sharding import PartitionSpec as P

F32, BF16, F16 = jnp.float32, jnp.bfloat16, jnp.float16
VMEM_LIMIT = 48 * 1024 * 1024


def slot_owner(total, capacity):
    slots = total * capacity
    first = lax.broadcasted_iota(jnp.int32, (slots, total), 1) * capacity
    slot = lax.broadcasted_iota(jnp.int32, (slots, total), 0)
    return ((slot >= first) & (slot < first + capacity)).astype(F32).astype(BF16)


def slot_offset(total, capacity, rows):
    slot = lax.broadcasted_iota(jnp.int32, (total * capacity, rows), 0).astype(F32)
    return slot - capacity * jnp.floor((slot + 0.5) * (1.0 / capacity))


def earlier_tokens(rows):
    earlier = lax.broadcasted_iota(jnp.int32, (rows, rows), 0)
    return (earlier < lax.broadcasted_iota(jnp.int32, (rows, rows), 1)).astype(F32).astype(BF16)


def places(ids_t, total, earlier):
    top, rows = ids_t.shape
    expert = lax.broadcasted_iota(jnp.int32, (total, rows), 0)
    named = [ids_t[k : k + 1, :] == expert for k in range(top)]
    member = functools.reduce(jnp.logical_or, named)
    count = jnp.dot(member.astype(F32).astype(BF16), earlier, preferred_element_type=F32)
    return jnp.where(member, count, -1.0).astype(BF16), named


def dispatch_kernel(total, capacity, ids_ref, tokens_ref, out_ref, ids, tokens, chunks, sems):
    parts, part = chunks.shape[0], chunks.shape[1]
    rows = tokens.shape[0]
    fetch_ids = pltpu.make_async_copy(ids_ref, ids, sems.at[0])
    fetch_tokens = pltpu.make_async_copy(tokens_ref, tokens, sems.at[1])
    fetch_ids.start()
    fetch_tokens.start()
    owner = slot_owner(total, capacity)
    offset = slot_offset(total, capacity, rows)
    earlier = earlier_tokens(rows)
    fetch_ids.wait()
    place, _ = places(ids[...], total, earlier)
    fetch_tokens.wait()
    held = tokens[...]
    sends = []
    for i in range(parts):
        own = slice(i * part, (i + 1) * part)
        wide = jnp.dot(owner[own], place, preferred_element_type=F32)
        taken = (wide == offset[own]).astype(F32).astype(BF16)
        chunks[i] = jnp.dot(taken, held, preferred_element_type=F32).astype(BF16)
        send = pltpu.make_async_copy(
            chunks.at[i], out_ref.at[pl.ds(i * part, part)], sems.at[2 + i]
        )
        send.start()
        sends.append(send)
    for send in sends:
        send.wait()


def weight_kernel(total, capacity, ids_ref, combine_ref, high_ref, low_ref):
    spread = slot_owner(total, capacity)
    place, named = places(ids_ref[...], total, earlier_tokens(ids_ref.shape[1]))
    wide = jnp.dot(spread, place, preferred_element_type=F32)
    taken = wide == slot_offset(total, capacity, ids_ref.shape[1])
    combine = combine_ref[...]
    weight = functools.reduce(
        jnp.add, [jnp.where(n, combine[k : k + 1, :], 0.0) for k, n in enumerate(named)]
    )
    high = weight.astype(BF16)
    low = (weight - high.astype(F32)).astype(BF16)
    for part, ref in ((high, high_ref), (low, low_ref)):
        wide = jnp.dot(spread, part, preferred_element_type=F32)
        ref[...] = jnp.where(taken, wide, 0.0).T.astype(BF16)


def beside_kernel(left_ref, right_ref, out_ref):
    width = left_ref.shape[1]
    out_ref[:, :width] = left_ref[...]
    out_ref[:, width:] = right_ref[...]


def select_kernel(capacity, *refs):
    out_ref = refs[-1]
    width = out_ref.shape[1]
    start = 0
    for outs_ref in refs[:-1]:
        rows, wide = outs_ref.shape
        here = wide // width
        block = here * capacity
        row = lax.broadcasted_iota(jnp.int32, (rows, width), 0).astype(F32)
        row = row - block * jnp.floor((row + 0.5) * (1.0 / block))
        out = outs_ref[:, :width]
        for e in range(1, here):
            out = jnp.where(row < e * capacity, out, outs_ref[:, e * width : (e + 1) * width])
        out_ref[start : start + rows] = out
        start += rows


def split_kernel(capacity, rows_ref, out_ref):
    here, width = out_ref.shape[1] // rows_ref.shape[1], rows_ref.shape[1]
    block = here * capacity
    row = lax.broadcasted_iota(jnp.int32, rows_ref.shape, 0).astype(F32)
    row = row - block * jnp.floor((row + 0.5) * (1.0 / block))
    rows = rows_ref[...]
    for e in range(here):
        own = (row >= e * capacity) & (row < (e + 1) * capacity)
        out_ref[:, e * width : (e + 1) * width] = jnp.where(own, rows, jnp.zeros((), BF16))


def mix_kernel(high_ref, low_ref, back_ref, out_ref):
    back = back_ref[...]
    out_ref[...] = (
        jnp.dot(high_ref[...], back, preferred_element_type=F32)
        + jnp.dot(low_ref[...], back, preferred_element_type=F32)
    ).astype(BF16)


def per_device(tokens, expert_ids, combine, gate_weight, up_weight, down_weight):
    n_cols = lax.axis_size("expert")
    rows, width = tokens.shape
    here, _, ff = gate_weight.shape
    capacity = rows * 5 // 32
    total = n_cols * here
    slots = total * capacity
    parts = 2
    ids_t = expert_ids.T
    params = pltpu.CompilerParams(vmem_limit_bytes=VMEM_LIMIT)
    outgoing = pl.pallas_call(
        functools.partial(dispatch_kernel, total, capacity),
        out_shape=jax.ShapeDtypeStruct((slots, width), BF16),
        in_specs=[pl.BlockSpec(memory_space=pltpu.HBM)] * 2,
        out_specs=pl.BlockSpec(memory_space=pltpu.HBM),
        scratch_shapes=[
            pltpu.VMEM(ids_t.shape, jnp.int32),
            pltpu.VMEM((rows, width), BF16),
            pltpu.VMEM((parts, slots // parts, width), BF16),
            pltpu.SemaphoreType.DMA((2 + parts,)),
        ],
    )(ids_t, tokens)
    high, low = pl.pallas_call(
        functools.partial(weight_kernel, total, capacity),
        out_shape=[jax.ShapeDtypeStruct((rows, slots), BF16)] * 2,
        compiler_params=params,
    )(ids_t, combine.T)
    block = here * capacity
    arrived = lax.all_to_all(
        outgoing.reshape(n_cols, block, width), "expert", split_axis=0, concat_axis=0, tiled=True
    ).reshape(slots, width)
    rows_in = pl.pallas_call(
        functools.partial(split_kernel, capacity),
        out_shape=jax.ShapeDtypeStruct((slots, here * width), BF16),
        compiler_params=params,
    )(arrived)

    halves = pl.pallas_call(
        beside_kernel,
        out_shape=jax.ShapeDtypeStruct((here * width, 2 * ff), BF16),
        compiler_params=params,
    )(gate_weight.reshape(here * width, ff), up_weight.reshape(here * width, ff))
    both = jnp.concatenate([down_weight[e] for e in range(here)], axis=1)

    def project(rows_part):
        part = jnp.dot(rows_part, halves, preferred_element_type=F32)
        return (part * 16.0).astype(F16)

    def expert_outs(sums):
        gate = sums[:, :ff].astype(F32) * (1.0 / 16.0)
        up = sums[:, ff:].astype(F32) * (1.0 / 16.0)
        hidden = (jax.nn.silu(gate) * up).astype(BF16)
        return jnp.dot(hidden, both, preferred_element_type=F32).astype(BF16)

    cut = n_cols * 11 // 16 * block
    sums = lax.psum((project(rows_in[:cut]), project(rows_in[cut:])), "dp")
    result = pl.pallas_call(
        functools.partial(select_kernel, capacity),
        out_shape=jax.ShapeDtypeStruct((slots, width), BF16),
        compiler_params=params,
    )(*[expert_outs(part) for part in sums])
    result, high, low = lax.optimization_barrier((result, high, low))
    returned = lax.all_to_all(
        result.reshape(n_cols, block, width), "expert", split_axis=0, concat_axis=0, tiled=True
    ).reshape(slots, width)
    return pl.pallas_call(
        mix_kernel,
        out_shape=jax.ShapeDtypeStruct((rows, width), BF16),
        compiler_params=params,
    )(high, low, returned)


def solution(mesh):
    placed = (
        P("expert", "dp"),
        P("expert", None),
        P("expert", None),
        P("expert", "dp", None),
        P("expert", "dp", None),
        P("expert", None, "dp"),
    )
    return jax.shard_map(
        per_device, mesh=mesh, in_specs=placed, out_specs=P("expert", "dp"), check_vma=False
    )
```

```python
import functools

import jax
import jax.numpy as jnp
from jax import lax
from jax.experimental import pallas as pl
from jax.experimental.pallas import tpu as pltpu
from jax.sharding import PartitionSpec as P

F32, BF16, F16 = jnp.float32, jnp.bfloat16, jnp.float16
VMEM_LIMIT = 48 * 1024 * 1024


def slot_owner(total, capacity):
    slots = total * capacity
    first = lax.broadcasted_iota(jnp.int32, (slots, total), 1) * capacity
    slot = lax.broadcasted_iota(jnp.int32, (slots, total), 0)
    return ((slot >= first) & (slot < first + capacity)).astype(F32).astype(BF16)


def slot_offset(total, capacity, rows):
    slot = lax.broadcasted_iota(jnp.int32, (total * capacity, rows), 0).astype(F32)
    return slot - capacity * jnp.floor((slot + 0.5) * (1.0 / capacity))


def earlier_tokens(rows):
    earlier = lax.broadcasted_iota(jnp.int32, (rows, rows), 0)
    return (earlier < lax.broadcasted_iota(jnp.int32, (rows, rows), 1)).astype(F32).astype(BF16)


def places(ids_t, total, earlier):
    top, rows = ids_t.shape
    expert = lax.broadcasted_iota(jnp.int32, (total, rows), 0)
    named = [ids_t[k : k + 1, :] == expert for k in range(top)]
    member = functools.reduce(jnp.logical_or, named)
    count = jnp.dot(member.astype(F32).astype(BF16), earlier, preferred_element_type=F32)
    return jnp.where(member, count, -1.0).astype(BF16), named


def dispatch_kernel(total, capacity, ids_ref, tokens_ref, out_ref, ids, tokens, chunks, sems):
    parts, part = chunks.shape[0], chunks.shape[1]
    rows = tokens.shape[0]
    fetch_ids = pltpu.make_async_copy(ids_ref, ids, sems.at[0])
    fetch_tokens = pltpu.make_async_copy(tokens_ref, tokens, sems.at[1])
    fetch_ids.start()
    fetch_tokens.start()
    owner = slot_owner(total, capacity)
    offset = slot_offset(total, capacity, rows)
    earlier = earlier_tokens(rows)
    fetch_ids.wait()
    place, _ = places(ids[...], total, earlier)
    fetch_tokens.wait()
    held = tokens[...]
    sends = []
    for i in range(parts):
        own = slice(i * part, (i + 1) * part)
        wide = jnp.dot(owner[own], place, preferred_element_type=F32)
        taken = (wide == offset[own]).astype(F32).astype(BF16)
        chunks[i] = jnp.dot(taken, held, preferred_element_type=F32).astype(BF16)
        send = pltpu.make_async_copy(
            chunks.at[i], out_ref.at[pl.ds(i * part, part)], sems.at[2 + i]
        )
        send.start()
        sends.append(send)
    for send in sends:
        send.wait()


def weight_kernel(total, capacity, ids_ref, combine_ref, high_ref, low_ref):
    spread = slot_owner(total, capacity)
    place, named = places(ids_ref[...], total, earlier_tokens(ids_ref.shape[1]))
    wide = jnp.dot(spread, place, preferred_element_type=F32)
    taken = wide == slot_offset(total, capacity, ids_ref.shape[1])
    combine = combine_ref[...]
    weight = functools.reduce(
        jnp.add, [jnp.where(n, combine[k : k + 1, :], 0.0) for k, n in enumerate(named)]
    )
    high = weight.astype(BF16)
    low = (weight - high.astype(F32)).astype(BF16)
    for part, ref in ((high, high_ref), (low, low_ref)):
        wide = jnp.dot(spread, part, preferred_element_type=F32)
        ref[...] = jnp.where(taken, wide, 0.0).T.astype(BF16)


def beside_kernel(left_ref, right_ref, out_ref):
    width = left_ref.shape[1]
    out_ref[:, :width] = left_ref[...]
    out_ref[:, width:] = right_ref[...]


def select_kernel(capacity, *refs):
    out_ref = refs[-1]
    width = out_ref.shape[1]
    start = 0
    for outs_ref in refs[:-1]:
        rows, wide = outs_ref.shape
        here = wide // width
        block = here * capacity
        row = lax.broadcasted_iota(jnp.int32, (rows, width), 0).astype(F32)
        row = row - block * jnp.floor((row + 0.5) * (1.0 / block))
        out = outs_ref[:, :width]
        for e in range(1, here):
            out = jnp.where(row < e * capacity, out, outs_ref[:, e * width : (e + 1) * width])
        out_ref[start : start + rows] = out
        start += rows


def split_kernel(capacity, rows_ref, out_ref):
    here, width = out_ref.shape[1] // rows_ref.shape[1], rows_ref.shape[1]
    block = here * capacity
    row = lax.broadcasted_iota(jnp.int32, rows_ref.shape, 0).astype(F32)
    row = row - block * jnp.floor((row + 0.5) * (1.0 / block))
    rows = rows_ref[...]
    for e in range(here):
        own = (row >= e * capacity) & (row < (e + 1) * capacity)
        out_ref[:, e * width : (e + 1) * width] = jnp.where(own, rows, jnp.zeros((), BF16))


def mix_kernel(high_ref, low_ref, back_ref, out_ref):
    back = back_ref[...]
    out_ref[...] = (
        jnp.dot(high_ref[...], back, preferred_element_type=F32)
        + jnp.dot(low_ref[...], back, preferred_element_type=F32)
    ).astype(BF16)


def per_device(tokens, expert_ids, combine, gate_weight, up_weight, down_weight):
    n_cols = lax.axis_size("expert")
    rows, width = tokens.shape
    here, _, ff = gate_weight.shape
    capacity = rows * 5 // 32
    total = n_cols * here
    slots = total * capacity
    parts = 2
    ids_t = expert_ids.T
    params = pltpu.CompilerParams(vmem_limit_bytes=VMEM_LIMIT)
    outgoing = pl.pallas_call(
        functools.partial(dispatch_kernel, total, capacity),
        out_shape=jax.ShapeDtypeStruct((slots, width), BF16),
        in_specs=[pl.BlockSpec(memory_space=pltpu.HBM)] * 2,
        out_specs=pl.BlockSpec(memory_space=pltpu.HBM),
        scratch_shapes=[
            pltpu.VMEM(ids_t.shape, jnp.int32),
            pltpu.VMEM((rows, width), BF16),
            pltpu.VMEM((parts, slots // parts, width), BF16),
            pltpu.SemaphoreType.DMA((2 + parts,)),
        ],
    )(ids_t, tokens)
    high, low = pl.pallas_call(
        functools.partial(weight_kernel, total, capacity),
        out_shape=[jax.ShapeDtypeStruct((rows, slots), BF16)] * 2,
        compiler_params=params,
    )(ids_t, combine.T)
    block = here * capacity
    arrived = lax.all_to_all(
        outgoing.reshape(n_cols, block, width), "expert", split_axis=0, concat_axis=0, tiled=True
    ).reshape(slots, width)
    rows_in = pl.pallas_call(
        functools.partial(split_kernel, capacity),
        out_shape=jax.ShapeDtypeStruct((slots, here * width), BF16),
        compiler_params=params,
    )(arrived)

    halves = pl.pallas_call(
        beside_kernel,
        out_shape=jax.ShapeDtypeStruct((here * width, 2 * ff), BF16),
        compiler_params=params,
    )(gate_weight.reshape(here * width, ff), up_weight.reshape(here * width, ff))
    both = jnp.concatenate([down_weight[e] for e in range(here)], axis=1)

    def project(rows_part):
        part = jnp.dot(rows_part, halves, preferred_element_type=F32)
        return (part * 16.0).astype(F16)

    def expert_outs(sums):
        gate = sums[:, :ff].astype(F32) * (1.0 / 16.0)
        up = sums[:, ff:].astype(F32) * (1.0 / 16.0)
        hidden = (jax.nn.silu(gate) * up).astype(BF16)
        return jnp.dot(hidden, both, preferred_element_type=F32).astype(BF16)

    cut = n_cols * 12 // 16 * block
    sums = lax.psum((project(rows_in[:cut]), project(rows_in[cut:])), "dp")
    result = pl.pallas_call(
        functools.partial(select_kernel, capacity),
        out_shape=jax.ShapeDtypeStruct((slots, width), BF16),
        compiler_params=params,
    )(*[expert_outs(part) for part in sums])
    result, high, low = lax.optimization_barrier((result, high, low))
    returned = lax.all_to_all(
        result.reshape(n_cols, block, width), "expert", split_axis=0, concat_axis=0, tiled=True
    ).reshape(slots, width)
    return pl.pallas_call(
        mix_kernel,
        out_shape=jax.ShapeDtypeStruct((rows, width), BF16),
        compiler_params=params,
    )(high, low, returned)


def solution(mesh):
    placed = (
        P("expert", "dp"),
        P("expert", None),
        P("expert", None),
        P("expert", "dp", None),
        P("expert", "dp", None),
        P("expert", None, "dp"),
    )
    return jax.shard_map(
        per_device, mesh=mesh, in_specs=placed, out_specs=P("expert", "dp"), check_vma=False
    )
```

```python
import functools

import jax
import jax.numpy as jnp
from jax import lax
from jax.experimental import pallas as pl
from jax.experimental.pallas import tpu as pltpu
from jax.sharding import PartitionSpec as P

F32, BF16, F16 = jnp.float32, jnp.bfloat16, jnp.float16
VMEM_LIMIT = 48 * 1024 * 1024


def slot_owner(total, capacity):
    slots = total * capacity
    first = lax.broadcasted_iota(jnp.int32, (slots, total), 1) * capacity
    slot = lax.broadcasted_iota(jnp.int32, (slots, total), 0)
    return ((slot >= first) & (slot < first + capacity)).astype(F32).astype(BF16)


def slot_offset(total, capacity, rows):
    slot = lax.broadcasted_iota(jnp.int32, (total * capacity, rows), 0).astype(F32)
    return slot - capacity * jnp.floor((slot + 0.5) * (1.0 / capacity))


def earlier_tokens(rows):
    earlier = lax.broadcasted_iota(jnp.int32, (rows, rows), 0)
    return (earlier < lax.broadcasted_iota(jnp.int32, (rows, rows), 1)).astype(F32).astype(BF16)


def places(ids_t, total, earlier):
    top, rows = ids_t.shape
    expert = lax.broadcasted_iota(jnp.int32, (total, rows), 0)
    named = [ids_t[k : k + 1, :] == expert for k in range(top)]
    member = functools.reduce(jnp.logical_or, named)
    count = jnp.dot(member.astype(F32).astype(BF16), earlier, preferred_element_type=F32)
    return jnp.where(member, count, -1.0).astype(BF16), named


def dispatch_kernel(total, capacity, ids_ref, tokens_ref, out_ref, ids, tokens, chunks, sems):
    parts, part = chunks.shape[0], chunks.shape[1]
    rows = tokens.shape[0]
    fetch_ids = pltpu.make_async_copy(ids_ref, ids, sems.at[0])
    fetch_tokens = pltpu.make_async_copy(tokens_ref, tokens, sems.at[1])
    fetch_ids.start()
    fetch_tokens.start()
    owner = slot_owner(total, capacity)
    offset = slot_offset(total, capacity, rows)
    earlier = earlier_tokens(rows)
    fetch_ids.wait()
    place, _ = places(ids[...], total, earlier)
    fetch_tokens.wait()
    held = tokens[...]
    sends = []
    for i in range(parts):
        own = slice(i * part, (i + 1) * part)
        wide = jnp.dot(owner[own], place, preferred_element_type=F32)
        taken = (wide == offset[own]).astype(F32).astype(BF16)
        chunks[i] = jnp.dot(taken, held, preferred_element_type=F32).astype(BF16)
        send = pltpu.make_async_copy(
            chunks.at[i], out_ref.at[pl.ds(i * part, part)], sems.at[2 + i]
        )
        send.start()
        sends.append(send)
    for send in sends:
        send.wait()


def weight_kernel(total, capacity, ids_ref, combine_ref, high_ref, low_ref):
    spread = slot_owner(total, capacity)
    place, named = places(ids_ref[...], total, earlier_tokens(ids_ref.shape[1]))
    wide = jnp.dot(spread, place, preferred_element_type=F32)
    taken = wide == slot_offset(total, capacity, ids_ref.shape[1])
    combine = combine_ref[...]
    weight = functools.reduce(
        jnp.add, [jnp.where(n, combine[k : k + 1, :], 0.0) for k, n in enumerate(named)]
    )
    high = weight.astype(BF16)
    low = (weight - high.astype(F32)).astype(BF16)
    for part, ref in ((high, high_ref), (low, low_ref)):
        wide = jnp.dot(spread, part, preferred_element_type=F32)
        ref[...] = jnp.where(taken, wide, 0.0).T.astype(BF16)


def beside_kernel(*refs):
    out_ref = refs[-1]
    width = refs[0].shape[1]
    for i, ref in enumerate(refs[:-1]):
        out_ref[:, i * width : (i + 1) * width] = ref[...]


def select_kernel(capacity, *refs):
    out_ref = refs[-1]
    width = out_ref.shape[1]
    start = 0
    for outs_ref in refs[:-1]:
        rows, wide = outs_ref.shape
        here = wide // width
        block = here * capacity
        row = lax.broadcasted_iota(jnp.int32, (rows, width), 0).astype(F32)
        row = row - block * jnp.floor((row + 0.5) * (1.0 / block))
        out = outs_ref[:, :width]
        for e in range(1, here):
            out = jnp.where(row < e * capacity, out, outs_ref[:, e * width : (e + 1) * width])
        out_ref[start : start + rows] = out
        start += rows


def split_kernel(capacity, rows_ref, out_ref):
    here, width = out_ref.shape[1] // rows_ref.shape[1], rows_ref.shape[1]
    block = here * capacity
    row = lax.broadcasted_iota(jnp.int32, rows_ref.shape, 0).astype(F32)
    row = row - block * jnp.floor((row + 0.5) * (1.0 / block))
    rows = rows_ref[...]
    for e in range(here):
        own = (row >= e * capacity) & (row < (e + 1) * capacity)
        out_ref[:, e * width : (e + 1) * width] = jnp.where(own, rows, jnp.zeros((), BF16))


def mix_kernel(high_ref, low_ref, back_ref, out_ref):
    back = back_ref[...]
    out_ref[...] = (
        jnp.dot(high_ref[...], back, preferred_element_type=F32)
        + jnp.dot(low_ref[...], back, preferred_element_type=F32)
    ).astype(BF16)


def per_device(tokens, expert_ids, combine, gate_weight, up_weight, down_weight):
    n_cols = lax.axis_size("expert")
    rows, width = tokens.shape
    here, _, ff = gate_weight.shape
    capacity = rows * 5 // 32
    total = n_cols * here
    slots = total * capacity
    parts = 2
    ids_t = expert_ids.T
    params = pltpu.CompilerParams(vmem_limit_bytes=VMEM_LIMIT)
    outgoing = pl.pallas_call(
        functools.partial(dispatch_kernel, total, capacity),
        out_shape=jax.ShapeDtypeStruct((slots, width), BF16),
        in_specs=[pl.BlockSpec(memory_space=pltpu.HBM)] * 2,
        out_specs=pl.BlockSpec(memory_space=pltpu.HBM),
        scratch_shapes=[
            pltpu.VMEM(ids_t.shape, jnp.int32),
            pltpu.VMEM((rows, width), BF16),
            pltpu.VMEM((parts, slots // parts, width), BF16),
            pltpu.SemaphoreType.DMA((2 + parts,)),
        ],
    )(ids_t, tokens)
    high, low = pl.pallas_call(
        functools.partial(weight_kernel, total, capacity),
        out_shape=[jax.ShapeDtypeStruct((rows, slots), BF16)] * 2,
        compiler_params=params,
    )(ids_t, combine.T)
    block = here * capacity
    arrived = lax.all_to_all(
        outgoing.reshape(n_cols, block, width), "expert", split_axis=0, concat_axis=0, tiled=True
    ).reshape(slots, width)
    rows_in = pl.pallas_call(
        functools.partial(split_kernel, capacity),
        out_shape=jax.ShapeDtypeStruct((slots, here * width), BF16),
        compiler_params=params,
    )(arrived)

    halves = pl.pallas_call(
        beside_kernel,
        out_shape=jax.ShapeDtypeStruct((here * width, 2 * ff), BF16),
        compiler_params=params,
    )(gate_weight.reshape(here * width, ff), up_weight.reshape(here * width, ff))
    both = pl.pallas_call(
        beside_kernel,
        out_shape=jax.ShapeDtypeStruct((ff, here * width), BF16),
        compiler_params=params,
    )(*[down_weight[e] for e in range(here)])

    def project(rows_part):
        part = jnp.dot(rows_part, halves, preferred_element_type=F32)
        return (part * 16.0).astype(F16)

    def expert_outs(sums):
        gate = sums[:, :ff].astype(F32) * (1.0 / 16.0)
        up = sums[:, ff:].astype(F32) * (1.0 / 16.0)
        hidden = (jax.nn.silu(gate) * up).astype(BF16)
        return jnp.dot(hidden, both, preferred_element_type=F32).astype(BF16)

    cut = n_cols * 12 // 16 * block
    sums = lax.psum((project(rows_in[:cut]), project(rows_in[cut:])), "dp")
    result = pl.pallas_call(
        functools.partial(select_kernel, capacity),
        out_shape=jax.ShapeDtypeStruct((slots, width), BF16),
        compiler_params=params,
    )(*[expert_outs(part) for part in sums])
    result, high, low = lax.optimization_barrier((result, high, low))
    returned = lax.all_to_all(
        result.reshape(n_cols, block, width), "expert", split_axis=0, concat_axis=0, tiled=True
    ).reshape(slots, width)
    return pl.pallas_call(
        mix_kernel,
        out_shape=jax.ShapeDtypeStruct((rows, width), BF16),
        compiler_params=params,
    )(high, low, returned)


def solution(mesh):
    placed = (
        P("expert", "dp"),
        P("expert", None),
        P("expert", None),
        P("expert", "dp", None),
        P("expert", "dp", None),
        P("expert", None, "dp"),
    )
    return jax.shard_map(
        per_device, mesh=mesh, in_specs=placed, out_specs=P("expert", "dp"), check_vma=False
    )
```
